512 devices in a mesh: ctx: 64 (over x, y, z_lo), head: 8 (over z_hi, core).
Axes of the slice: x: 4, y: 8, z: 8 (z_hi: 4, z_lo: 2; z = z_hi * 2 + z_lo), core: 2. Of those that a mesh axis runs over, the one named last changes fastest.
Arguments:
- query_in: bfloat16 [16384, 64, 128], P(('ctx', 'head')), may hold values from -8 to 8
- key_in: bfloat16 [16384, 8, 128], P(('ctx', 'head')), may hold values from -8 to 8
- value_in: bfloat16 [16384, 8, 128], P(('ctx', 'head')), may hold values from -6 to 6
- grad_out: bfloat16 [16384, 64, 128], P(('ctx', 'head')), may hold values from -6 to 6
- doc_lengths: int32 [32], replicated, may hold values from 1 to 1024, 16384 in all
Outputs:
- attn_out: bfloat16 [16384, 64, 128], P(('ctx', 'head'))
- grad_query: bfloat16 [16384, 64, 128], P(('ctx', 'head'))
- grad_key: bfloat16 [16384, 8, 128], P(('ctx', 'head'))
- grad_value: bfloat16 [16384, 8, 128], P(('ctx', 'head'))
The draws below stay inside these ranges and needn't reach their ends.
Inputs may be any that keep to these rules, and one draw needn't show every extreme that they name: `doc_lengths`: 32 documents whose lengths sum to 16384; the longest has exactly 1024 tokens.
All inputs are finite; a program needn't handle non-finite values.
Results may differ from the reference program's by a relative error of at most 0.022.
Values may be sent and summed in bfloat16 or wider, within the bound.
No kernel may reach another device: no remote copies, remote signals or barrier semaphores. Data moves between devices by JAX's collectives and lax.ppermute only.
A program may use at most 64 MiB of HBM per device.

```python
import math
import jax
import jax.numpy as jnp
import numpy as np
from jax import lax

QH = 64
KVH = 8
HD = 128
TOK_DEV = 256
DOC_MOST = 1024
CONTEXT = 16384
DOCS = 32


def draw_query_in(key, part):
    key = jax.random.fold_in(key, 1)
    normal_part = jax.random.normal(key, (CONTEXT, QH, HD), jnp.float32)
    return jnp.clip(normal_part, -8.0, 8.0).astype(jnp.bfloat16)


def draw_key_in(key, part):
    key = jax.random.fold_in(key, 2)
    normal_part = jax.random.normal(key, (CONTEXT, KVH, HD), jnp.float32)
    return jnp.clip(normal_part, -8.0, 8.0).astype(jnp.bfloat16)


def shard_levels(stream_key, shape, pieces, low, high):
    level = 1.0
    for axis_at, blocks in pieces:
        heights = jax.random.uniform(jax.random.fold_in(jax.random.fold_in(stream_key, 6), axis_at), (blocks,), jnp.float32, low / len(pieces), high / len(pieces))
        level = level * jnp.repeat(jnp.exp(heights), shape[axis_at] // blocks).reshape((-1,) + (1,) * (len(shape) - 1 - axis_at))
    return level


def split_up(count, total, most, slope):
    loads = [(1 << 20) // math.isqrt(standing ** slope) + 1 for standing in range(2, count + 1)]
    spare, counts = total - most - (count - 1), [1] * (count - 1)
    while spare > 0:
        free = [i for i in range(count - 1) if counts[i] < most]
        whole, left = sum([loads[i] for i in free]), spare
        for i in free:
            more = min(most - counts[i], max(1, left * loads[i] // whole), spare)
            counts[i] = counts[i] + more
            spare = spare - more
    return np.array([most] + counts)


def uneven(key, amount, total, most, lean):
    if amount == 2:
        one = jax.random.randint(key, (), max(1, total - most), min(most, total - 1) + 1)
        return jnp.stack([one, total - one])
    tallies = jnp.asarray(split_up(amount, total, most, lean), jnp.int32)
    couples = (amount - 1) // 2
    source_of, sink = tallies[1:1 + 2 * couples:2], tallies[2:2 + 2 * couples:2]
    room = jnp.minimum(source_of - 1, most - sink)
    passed = jax.random.randint(jax.random.fold_in(key, 1), (couples,), 0, 1 << 20) % (room + 1)
    tallies = tallies.at[1:1 + 2 * couples:2].set(source_of - passed).at[2:2 + 2 * couples:2].set(sink + passed)
    return tallies[jax.random.permutation(jax.random.fold_in(key, 2), amount)]


def scatter_about(stream_key, extent, spread, bound, shards=(), kind=jnp.bfloat16):
    entries = spread * jax.random.normal(stream_key, extent, jnp.float32)
    if shards:
        entries = entries * shard_levels(stream_key, extent, shards, -0.22, 0.18)
    return jnp.clip(entries, -bound, bound).astype(kind)


def setup_inputs(seed: int = 0) -> dict:
    seeds = jax.random.split(jax.random.key(seed), 6)
    query_in = draw_query_in(jax.random.fold_in(seeds[5], 71), 0)
    key_in = draw_key_in(jax.random.fold_in(seeds[5], 71), 0)
    value_in = scatter_about(seeds[2], (CONTEXT, KVH, HD), 1.0, 6.0, ((0, 512),))
    grad_out = scatter_about(seeds[3], (CONTEXT, QH, HD), 1.0, 6.0, ((0, 512),))
    doc_lengths = uneven(seeds[4], DOCS, CONTEXT, DOC_MOST, 2).astype(jnp.int32)
    return dict(query_in=query_in, key_in=key_in, value_in=value_in, grad_out=grad_out, doc_lengths=doc_lengths)


def reference(query_in, key_in, value_in, grad_out, doc_lengths):
    group_size = QH // KVH
    score_scale = HD ** -0.5
    window = DOC_MOST + TOK_DEV
    doc_ends = jnp.cumsum(doc_lengths).astype(jnp.int32)
    positions = jnp.arange(CONTEXT, dtype=jnp.int32)
    segment = jnp.sum((doc_ends[None, :] <= positions[:, None]).astype(jnp.int32), axis=1).astype(jnp.int32)
    segment_pad = jnp.concatenate([jnp.full((DOC_MOST,), -1, jnp.int32), segment])
    key_pad = jnp.concatenate([jnp.zeros((DOC_MOST, KVH, HD), key_in.dtype), key_in])
    value_pad = jnp.concatenate([jnp.zeros((DOC_MOST, KVH, HD), value_in.dtype), value_in])

    def one_block(carried, block_index):
        grad_k_acc, grad_v_acc = carried
        block_start = (block_index * TOK_DEV).astype(jnp.int32)
        q_block = lax.dynamic_slice_in_dim(query_in, block_start, TOK_DEV, 0).astype(jnp.float32).reshape(TOK_DEV, KVH, group_size, HD)
        g_block = lax.dynamic_slice_in_dim(grad_out, block_start, TOK_DEV, 0).astype(jnp.float32).reshape(TOK_DEV, KVH, group_size, HD)
        k_window = lax.dynamic_slice_in_dim(key_pad, block_start, window, 0).astype(jnp.float32)
        v_window = lax.dynamic_slice_in_dim(value_pad, block_start, window, 0).astype(jnp.float32)
        q_place = block_start + jnp.arange(TOK_DEV, dtype=jnp.int32)
        k_place = block_start - DOC_MOST + jnp.arange(window, dtype=jnp.int32)
        q_segment = lax.dynamic_slice_in_dim(segment, block_start, TOK_DEV, 0)
        k_segment = lax.dynamic_slice_in_dim(segment_pad, block_start, window, 0)
        visible = (q_segment[:, None] == k_segment[None, :]) & (k_place[None, :] <= q_place[:, None]) & (k_place[None, :] >= 0)
        scores = jnp.einsum("tkgd,skd->kgts", q_block, k_window) * score_scale
        masked = jnp.where(visible[None, None], scores, -1e30)
        row_top = jnp.max(masked, axis=-1)
        log_total = row_top + jnp.log(jnp.sum(jnp.exp(masked - row_top[..., None]), axis=-1))
        weights = jnp.exp(masked - log_total[..., None])
        weights_b = lax.optimization_barrier(weights.astype(jnp.bfloat16)).astype(jnp.float32)
        out_float = jnp.einsum("kgts,skd->tkgd", weights_b, v_window)
        out_round = lax.optimization_barrier(out_float.astype(jnp.bfloat16))
        drift = jnp.sum(g_block * out_round.astype(jnp.float32), axis=-1)
        dprob = jnp.einsum("tkgd,skd->kgts", g_block, v_window)
        dscore = weights * (dprob - jnp.transpose(drift, (1, 2, 0))[..., None])
        dscore_b = lax.optimization_barrier(dscore.astype(jnp.bfloat16)).astype(jnp.float32)
        grad_q = score_scale * jnp.einsum("kgts,skd->tkgd", dscore_b, k_window)
        grad_k = score_scale * jnp.einsum("kgts,tkgd->skd", dscore_b, q_block)
        grad_v = jnp.einsum("kgts,tkgd->skd", weights_b, g_block)
        old_k = lax.dynamic_slice_in_dim(grad_k_acc, block_start, window, 0)
        old_v = lax.dynamic_slice_in_dim(grad_v_acc, block_start, window, 0)
        grad_k_acc = lax.dynamic_update_slice_in_dim(grad_k_acc, old_k + grad_k, block_start, 0)
        grad_v_acc = lax.dynamic_update_slice_in_dim(grad_v_acc, old_v + grad_v, block_start, 0)
        return (grad_k_acc, grad_v_acc), (out_round, grad_q.astype(jnp.bfloat16))

    start_acc = jnp.zeros((DOC_MOST + CONTEXT, KVH, HD), jnp.float32)
    block_ids = jnp.arange(CONTEXT // TOK_DEV, dtype=jnp.int32)
    (grad_k_acc, grad_v_acc), (out_blocks, grad_q_blocks) = lax.scan(one_block, (start_acc, start_acc), block_ids)
    attn_out = out_blocks.reshape(CONTEXT, QH, HD)
    grad_query = grad_q_blocks.reshape(CONTEXT, QH, HD)
    grad_key = grad_k_acc[DOC_MOST:].astype(jnp.bfloat16)
    grad_value = grad_v_acc[DOC_MOST:].astype(jnp.bfloat16)
    return (attn_out, grad_query, grad_key, grad_value)
```

```python
import functools
import math

import jax
import jax.numpy as jnp
from jax import lax
from jax.experimental import pallas as pl
from jax.experimental.pallas import tpu as pltpu
from jax.sharding import Mesh
from jax.sharding import PartitionSpec as P

AXES = ("x", "y", "l", "h", "c")
SIZES = (4, 8, 2, 4, 2)
RING = ("l", "h")
COLUMNS = ("x", "y")

HD = 128
KVH = 8
GROUP = 8
TOK = 32
COL = 512
REACH = 2
KEYS = (REACH + 1) * COL
PIECE = TOK * GROUP
TILE = 128
PAIR = 2
ROWS = PAIR * PIECE
BLOCKS = KVH // PAIR
SCALE = HD**-0.5
SCALE2 = SCALE * math.log2(math.e)
NEG = -1e30

F32 = jnp.float32
BF16 = jnp.bfloat16
VMEM = pl.BlockSpec(memory_space=pltpu.VMEM)
SMEM = pl.BlockSpec(memory_space=pltpu.SMEM)
NT = (((1,), (1,)), ((), ()))
TN = (((0,), (0,)), ((), ()))
NN = (((1,), (0,)), ((), ()))


def dot(a, b, dims):
    return lax.dot_general(a, b, dims, preferred_element_type=F32)


def call(kernel, outs, ins, scratch, name, flops=0, nbytes=1 << 20):
    return pl.pallas_call(
        kernel,
        out_shape=outs,
        in_specs=ins,
        out_specs=[VMEM] * len(outs),
        scratch_shapes=scratch,
        compiler_params=pltpu.CompilerParams(vmem_limit_bytes=48 << 20),
        cost_estimate=pl.CostEstimate(flops=flops, bytes_accessed=nbytes, transcendentals=0),
        name=name,
    )


def shape(*dims, dtype=BF16):
    return jax.ShapeDtypeStruct(dims, dtype)


def put_heads(x_ref, out_ref):
    for pair in range(KVH // 2):
        both = x_ref[:, pair * 2 * GROUP : (pair + 1) * 2 * GROUP, :].astype(F32)
        for part in range(2):
            half = both[:, part * GROUP : (part + 1) * GROUP, :]
            out_ref[2 * pair + part, 0:PIECE, :] = half.reshape(PIECE, HD).astype(BF16)


def take_heads(x_ref, out_ref):
    for pair in range(KVH // 2):
        halves = [
            x_ref[2 * pair + part, 0:PIECE, :].astype(F32).reshape(TOK, GROUP, HD) for part in range(2)
        ]
        out_ref[:, pair * 2 * GROUP : (pair + 1) * 2 * GROUP, :] = jnp.concatenate(halves, axis=1).astype(
            BF16
        )


def pack_qkv(q_ref, k_ref, v_ref, out_ref, wide):
    put_heads(q_ref, out_ref)
    for at, ref in ((0, k_ref), (1, v_ref)):
        wide[...] = ref[...].astype(F32).reshape(TOK * KVH, HD)
        for j in range(KVH):
            out_ref[j, PIECE + at * TOK : PIECE + (at + 1) * TOK, :] = wide[
                pl.ds(j, TOK, stride=KVH), :
            ].astype(BF16)


def pack_g(g_ref, out_ref):
    put_heads(g_ref, out_ref)


def unpack_o(x_ref, out_ref):
    take_heads(x_ref, out_ref)


def unpack_grads(x_ref, q_ref, k_ref, v_ref, wide):
    take_heads(x_ref, q_ref)
    for at, ref in ((0, k_ref), (1, v_ref)):
        for j in range(KVH):
            wide[pl.ds(j, TOK, stride=KVH), :] = x_ref[
                j, PIECE + at * TOK : PIECE + (at + 1) * TOK, :
            ].astype(F32)
        ref[...] = wide[...].reshape(TOK, KVH, HD).astype(BF16)


def visible(start, place, tile):
    index = tile * TILE + lax.broadcasted_iota(jnp.int32, (TILE, ROWS), 0)
    return (index >= start) & (index <= place)


def rows_of(ref, block):
    return ref[pl.ds(block * PAIR, PAIR), 0:PIECE, :].reshape(ROWS, HD)


def place_of(block, core):
    row = lax.broadcasted_iota(jnp.int32, (1, ROWS), 1)
    return REACH * COL + block * (PAIR * 2 * TOK) + (row // PIECE) * (2 * TOK) + core * TOK + (row % PIECE) // GROUP


def first_tile(low_ref, block):
    return low_ref[block] // TILE


def last_tile(block):
    return (REACH * COL + (block + 1) * (PAIR * 2 * TOK) - 1) // TILE


def forward(low_ref, core_ref, a_ref, start_ref, own_ref, other_ref, old_ref, other_old_ref,
            out_ref, stat_ref, keys, values, scores, total, top):
    core = core_ref[0]
    for column in range(REACH + 1):
        for piece in range(KVH):
            base = (REACH - column) * COL + piece * 2 * TOK
            for ref, old, which in ((own_ref, old_ref, core), (other_ref, other_old_ref, 1 - core)):
                at = pl.ds(pl.multiple_of(base + which * TOK, TOK), TOK)
                got = ref[piece] if column == 0 else old[column - 1, piece]
                keys[at, :] = got[0:TOK]
                values[at, :] = got[TOK : 2 * TOK]

    def one_block(block, _):
        rows = rows_of(a_ref, block)
        start = start_ref[block]
        place = place_of(block, core)
        first, last = first_tile(low_ref, block), last_tile(block)
        top[...] = jnp.full(top.shape, NEG, F32)

        def score(tile, _):
            at = pl.ds(pl.multiple_of(tile * TILE, TILE), TILE)
            s = dot(keys[at, :], rows, NT)
            s = jnp.where(visible(start, place, tile), s, NEG)
            scores[at, :] = s
            top[...] = jnp.maximum(top[...], jnp.max(s.reshape(TILE // 8, 8, ROWS), axis=0))
            return 0

        lax.fori_loop(first, last + 1, score, 0)
        row_top = jnp.max(top[...], axis=0, keepdims=True) * SCALE2
        top[...] = jnp.zeros(top.shape, F32)
        total[...] = jnp.zeros(total.shape, F32)

        def weigh(tile, _):
            at = pl.ds(pl.multiple_of(tile * TILE, TILE), TILE)
            p = jnp.exp2(scores[at, :] * SCALE2 - row_top)
            top[...] += jnp.sum(p.reshape(TILE // 8, 8, ROWS), axis=0)
            total[...] += dot(values[at, :], p.astype(BF16), TN)
            return 0

        lax.fori_loop(first, last + 1, weigh, 0)
        row_sum = jnp.sum(top[...], axis=0, keepdims=True)
        stat_ref[block] = row_top + jnp.log2(row_sum)
        out = jnp.transpose(total[...] / row_sum)
        out_ref[pl.ds(block * PAIR, PAIR)] = out.astype(BF16).reshape(PAIR, PIECE, HD)
        return 0

    lax.fori_loop(0, BLOCKS, one_block, 0)


def backward(low_ref, core_ref, a_ref, g_ref, o_ref, start_ref, stat_ref, own_ref, other_ref, old_ref, other_old_ref,
             dq_ref, mine_ref, theirs_ref, keys, values, dk, dv, total):
    core = core_ref[0]
    for column in range(REACH + 1):
        for piece in range(KVH):
            base = (REACH - column) * COL + piece * 2 * TOK
            for ref, old, which in ((own_ref, old_ref, core), (other_ref, other_old_ref, 1 - core)):
                at = pl.ds(pl.multiple_of(base + which * TOK, TOK), TOK)
                got = ref[piece] if column == 0 else old[column - 1, piece]
                keys[at, :] = got[0:TOK]
                values[at, :] = got[TOK : 2 * TOK]
    dk[...] = jnp.zeros(dk.shape, F32)
    dv[...] = jnp.zeros(dv.shape, F32)

    def one_block(block, _):
        rows = rows_of(a_ref, block)
        grads = rows_of(g_ref, block)
        outs = rows_of(o_ref, block)
        start = start_ref[block]
        stat = stat_ref[block]
        place = place_of(block, core)
        prod = grads.astype(F32) * outs.astype(F32)
        high = prod.astype(BF16)
        low = (prod - high.astype(F32)).astype(BF16)
        ones = jnp.ones((8, HD), BF16)
        drift = (dot(ones, high, NT) + dot(ones, low, NT))[0:1]
        total[...] = jnp.zeros(total.shape, F32)

        def step(tile, _):
            at = pl.ds(pl.multiple_of(tile * TILE, TILE), TILE)
            key, value = keys[at, :], values[at, :]
            s = dot(key, rows, NT)
            dp = dot(value, grads, NT)
            p = jnp.where(visible(start, place, tile), jnp.exp2(s * SCALE2 - stat), 0.0)
            ds = (p * (dp - drift)).astype(BF16)
            dv[at, :] += dot(p.astype(BF16), grads, NN)
            dk[at, :] += dot(ds, rows, NN)
            total[...] += dot(key, ds, TN)
            return 0

        lax.fori_loop(first_tile(low_ref, block), last_tile(block) + 1, step, 0)
        dq = jnp.transpose(total[...] * SCALE)
        dq_ref[pl.ds(block * PAIR, PAIR)] = dq.astype(BF16).reshape(PAIR, PIECE, HD)
        return 0

    lax.fori_loop(0, BLOCKS, one_block, 0)
    for column in range(REACH + 1):
        for piece in range(KVH):
            base = (REACH - column) * COL + piece * 2 * TOK
            for ref, which in ((mine_ref, core), (theirs_ref, 1 - core)):
                at = pl.ds(pl.multiple_of(base + which * TOK, TOK), TOK)
                ref[column, piece, 0:TOK] = (dk[at, :] * SCALE).astype(ref.dtype)
                ref[column, piece, TOK : 2 * TOK] = dv[at, :].astype(ref.dtype)


def old_terms(mine_ref, got_ref, one_ref, two_ref):
    one_ref[...] = (mine_ref[1] + got_ref[1].astype(F32)).astype(BF16)
    two_ref[...] = (mine_ref[2] + got_ref[2].astype(F32)).astype(BF16)


def pack_grads(dq_ref, mine_ref, got_ref, one_ref, two_ref, out_ref):
    out_ref[:, 0:PIECE, :] = dq_ref[...]
    out_ref[:, PIECE : PIECE + 2 * TOK, :] = (
        mine_ref[0] + got_ref[0].astype(F32) + one_ref[...].astype(F32) + two_ref[...].astype(F32)
    ).astype(BF16)


def exchange(x):
    return lax.all_to_all(x, RING, split_axis=0, concat_axis=0, tiled=True)


def shifted(x, by):
    count = SIZES[0] * SIZES[1]
    return lax.ppermute(x, COLUMNS, [(i, (i + by) % count) for i in range(count)])


def swapped(x):
    return lax.ppermute(x, "c", [(0, 1), (1, 0)])


def shards(query_in, key_in, value_in, grad_out, doc_lengths):
    wide = TOK * GROUP
    packed = call(
        pack_qkv, [shape(KVH, PIECE + 2 * TOK, HD)], [VMEM] * 3, [pltpu.VMEM((TOK * KVH, HD), F32)], "pack_qkv"
    )(query_in, key_in, value_in)[0]
    a = exchange(packed)
    packed_g = call(pack_g, [shape(KVH, PIECE, HD)], [VMEM], [], "pack_g")(grad_out)[0]
    kv = a[:, PIECE:, :]
    old_one, old_two = shifted(kv, 1), shifted(kv, 2)
    other = swapped(kv)
    g = exchange(packed_g)
    old = jnp.stack([old_one, old_two])
    other_old = swapped(old)

    column = lax.axis_index(COLUMNS)
    core = lax.axis_index("c")
    ends = jnp.cumsum(doc_lengths)
    row = jnp.arange(ROWS, dtype=jnp.int32)
    piece = jnp.arange(BLOCKS, dtype=jnp.int32)[:, None] * PAIR + (row // PIECE)[None, :]
    place = column * COL + piece * (2 * TOK) + core * TOK + ((row % PIECE) // GROUP)[None, :]
    start = jnp.max(
        jnp.where(ends[:, None, None] <= place[None], ends[:, None, None], 0), axis=0
    )
    start = jnp.maximum(start - (column - REACH) * COL, 0).astype(jnp.int32)
    low = start[:, 0]
    start = start[:, None, :]
    core_in = core.astype(jnp.int32)[None]

    flops = 2 * BLOCKS * ROWS * 1024 * HD
    out, stat = call(
        forward,
        [shape(KVH, PIECE, HD), shape(BLOCKS, 1, ROWS, dtype=F32)],
        [SMEM] * 2 + [VMEM] * 6,
        [
            pltpu.VMEM((KEYS, HD), BF16),
            pltpu.VMEM((KEYS, HD), BF16),
            pltpu.VMEM((KEYS, ROWS), F32),
            pltpu.VMEM((HD, ROWS), F32),
            pltpu.VMEM((8, ROWS), F32),
        ],
        "attend",
        2 * flops,
    )(low, core_in, a, start, kv, other, old, other_old)
    out_back = exchange(out)
    dq, mine, theirs = call(
        backward,
        [
            shape(KVH, PIECE, HD),
            shape(REACH + 1, KVH, 2 * TOK, HD, dtype=F32),
            shape(REACH + 1, KVH, 2 * TOK, HD),
        ],
        [SMEM] * 2 + [VMEM] * 9,
        [
            pltpu.VMEM((KEYS, HD), BF16),
            pltpu.VMEM((KEYS, HD), BF16),
            pltpu.VMEM((KEYS, HD), F32),
            pltpu.VMEM((KEYS, HD), F32),
            pltpu.VMEM((HD, ROWS), F32),
        ],
        "gradients",
        5 * flops,
    )(low, core_in, a, g, out, start, stat, kv, other, old, other_old)
    got = swapped(theirs)
    term = shape(KVH, 2 * TOK, HD)
    one, two = call(old_terms, [term, term], [VMEM] * 2, [], "old_terms")(mine, got)
    back_one, back_two = shifted(one, -1), shifted(two, -2)
    packed_grads = call(pack_grads, [shape(KVH, PIECE + 2 * TOK, HD)], [VMEM] * 5, [], "pack_grads")(
        dq, mine, got, back_one, back_two
    )[0]
    grads_back = exchange(packed_grads)
    attn_out = call(unpack_o, [shape(TOK, KVH * GROUP, HD)], [VMEM], [], "unpack_o")(out_back)[0]
    grad_query, grad_key, grad_value = call(
        unpack_grads,
        [shape(TOK, KVH * GROUP, HD), shape(TOK, KVH, HD), shape(TOK, KVH, HD)],
        [VMEM],
        [pltpu.VMEM((TOK * KVH, HD), F32)],
        "unpack_grads",
    )(grads_back)
    return (attn_out, grad_query, grad_key, grad_value)


def solution(mesh):
    fine = Mesh(mesh.devices.reshape(SIZES), AXES)
    tokens = P(AXES, None, None)
    return jax.shard_map(
        shards,
        mesh=fine,
        in_specs=(tokens, tokens, tokens, tokens, P()),
        out_specs=(tokens, tokens, tokens, tokens),
        check_vma=False,
    )
```

```python
import math

import jax
import jax.numpy as jnp
from jax import lax
from jax.experimental import pallas as pl
from jax.experimental.pallas import tpu as pltpu
from jax.sharding import Mesh
from jax.sharding import PartitionSpec as P

AXES = ("x", "y", "l", "h", "c")
SIZES = (4, 8, 2, 4, 2)
RING = ("l", "h")
COLUMNS = ("x", "y")

HD = 128
KVH = 8
GROUP = 8
TOK = 32
COL = 512
REACH = 2
KEYS = (REACH + 1) * COL
PIECE = TOK * GROUP
TILE = 128
PAIR = 2
ROWS = PAIR * PIECE
BLOCKS = KVH // PAIR
WIN = 9
SCALE = HD**-0.5
SCALE2 = SCALE * math.log2(math.e)
NEG = -1e30

F32 = jnp.float32
BF16 = jnp.bfloat16
VMEM = pl.BlockSpec(memory_space=pltpu.VMEM)
SMEM = pl.BlockSpec(memory_space=pltpu.SMEM)
NT = (((1,), (1,)), ((), ()))
NN = (((1,), (0,)), ((), ()))


def dot(a, b, dims):
    return lax.dot_general(a, b, dims, preferred_element_type=F32)


def call(kernel, outs, ins, scratch, name, flops=0, nbytes=1 << 20):
    return pl.pallas_call(
        kernel,
        out_shape=outs,
        in_specs=ins,
        out_specs=[VMEM] * len(outs),
        scratch_shapes=scratch,
        compiler_params=pltpu.CompilerParams(vmem_limit_bytes=48 << 20),
        cost_estimate=pl.CostEstimate(flops=flops, bytes_accessed=nbytes, transcendentals=0),
        name=name,
    )


def shape(*dims, dtype=BF16):
    return jax.ShapeDtypeStruct(dims, dtype)


def put_heads(x_ref, out_ref, at):
    for pair in range(KVH // 2):
        both = x_ref[:, pair * 2 * GROUP : (pair + 1) * 2 * GROUP, :].astype(F32)
        for part in range(2):
            half = both[:, part * GROUP : (part + 1) * GROUP, :]
            out_ref[2 * pair + part, at : at + PIECE, :] = half.reshape(PIECE, HD).astype(BF16)


def take_heads(x_ref, at, out_ref):
    for pair in range(KVH // 2):
        halves = [
            x_ref[2 * pair + part, at : at + PIECE, :].astype(F32).reshape(TOK, GROUP, HD)
            for part in range(2)
        ]
        both = jnp.concatenate(halves, axis=1).astype(BF16)
        out_ref[:, pair * 2 * GROUP : (pair + 1) * 2 * GROUP, :] = both


def pack_kv(k_ref, v_ref, out_ref, wide):
    for at, ref in ((0, k_ref), (TOK, v_ref)):
        wide[...] = ref[...].astype(F32).reshape(TOK * KVH, HD)
        for j in range(KVH):
            out_ref[j, at : at + TOK, :] = wide[pl.ds(j, TOK, stride=KVH), :].astype(BF16)


def pack_qg(q_ref, g_ref, out_ref):
    put_heads(q_ref, out_ref, 0)
    put_heads(g_ref, out_ref, PIECE)


def unpack_od(x_ref, out_ref, dq_ref):
    take_heads(x_ref, 0, out_ref)
    take_heads(x_ref, PIECE, dq_ref)


def unpack_kv(x_ref, k_ref, v_ref, wide):
    for at, ref in ((0, k_ref), (TOK, v_ref)):
        for j in range(KVH):
            wide[pl.ds(j, TOK, stride=KVH), :] = x_ref[j, at : at + TOK, :].astype(F32)
        ref[...] = wide[...].reshape(TOK, KVH, HD).astype(BF16)


def attend(core_ref, qg_ref, start_ref, own_ref, other_ref, old_ref, other_old_ref,
           od_ref, mine_ref, theirs_ref,
           keys, values, keys_t, values_t, scores, probs, dscores, dk, dv):
    core = core_ref[0]
    for column in range(REACH + 1):
        for piece in range(KVH):
            base = (REACH - column) * COL + piece * 2 * TOK
            for ref, old, which in ((own_ref, old_ref, core), (other_ref, other_old_ref, 1 - core)):
                at = pl.ds(pl.multiple_of(base + which * TOK, TOK), TOK)
                got = ref[piece] if column == 0 else old[column - 1, piece]
                keys[at, :] = got[0:TOK]
                values[at, :] = got[TOK : 2 * TOK]
    for t in range(KEYS // TILE):
        at = slice(t * TILE, (t + 1) * TILE)
        keys_t[:, at] = jnp.transpose(keys[at, :])
        values_t[:, at] = jnp.transpose(values[at, :])
    dk[...] = jnp.zeros(dk.shape, F32)
    dv[...] = jnp.zeros(dv.shape, F32)
    index = lax.broadcasted_iota(jnp.int32, (TILE, ROWS), 0)
    row = lax.broadcasted_iota(jnp.int32, (1, ROWS), 1)
    inside = (row // PIECE) * (2 * TOK) + core * TOK + (row % PIECE) // GROUP

    def one_block(block, _):
        base = pl.multiple_of(block * TILE, TILE)
        window = pl.ds(base, WIN * TILE)
        q = qg_ref[pl.ds(block * PAIR, PAIR), 0:PIECE, :].reshape(ROWS, HD)
        g = qg_ref[pl.ds(block * PAIR, PAIR), PIECE : 2 * PIECE, :].reshape(ROWS, HD)
        start = start_ref[block] - base
        top = jnp.full((8, ROWS), NEG, F32)
        for t in range(WIN):
            s = dot(keys[pl.ds(base + t * TILE, TILE), :], q, NT)
            seen = index >= start - t * TILE
            if t == WIN - 1:
                seen = seen & (index <= inside)
            s = jnp.where(seen, s, NEG)
            scores[t * TILE : (t + 1) * TILE, :] = s
            top = jnp.maximum(top, jnp.max(s.reshape(TILE // 8, 8, ROWS), axis=0))
        row_top = jnp.max(top, axis=0, keepdims=True) * SCALE2
        sums = jnp.zeros((8, ROWS), F32)
        for t in range(WIN):
            p = jnp.exp2(scores[t * TILE : (t + 1) * TILE, :] * SCALE2 - row_top)
            sums = sums + jnp.sum(p.reshape(TILE // 8, 8, ROWS), axis=0)
            probs[t * TILE : (t + 1) * TILE, :] = p.astype(BF16)
        inv = 1.0 / jnp.sum(sums, axis=0, keepdims=True)
        out = jnp.transpose(dot(values_t[:, window], probs[...], NN) * inv).astype(BF16)
        od_ref[pl.ds(block * PAIR, PAIR), 0:PIECE, :] = out.reshape(PAIR, PIECE, HD)
        scaled = g.astype(F32) * jnp.transpose(jnp.broadcast_to(inv, (8, ROWS)))[:, 0:1]
        prod = scaled * out.astype(F32)
        high = prod.astype(BF16)
        low = (prod - high.astype(F32)).astype(BF16)
        ones = jnp.ones((8, HD), BF16)
        drift = (dot(ones, high, NT) + dot(ones, low, NT))[0:1]
        scaled = scaled.astype(BF16)
        for t in range(WIN):
            at = slice(t * TILE, (t + 1) * TILE)
            dp = dot(values[pl.ds(base + t * TILE, TILE), :], scaled, NT)
            dscores[at, :] = (dp - drift).astype(BF16) * probs[at, :]
        dv[window, :] += dot(probs[...], scaled, NN)
        dk[window, :] += dot(dscores[...], q, NN)
        dq = jnp.transpose(dot(keys_t[:, window], dscores[...], NN) * SCALE).astype(BF16)
        od_ref[pl.ds(block * PAIR, PAIR), PIECE : 2 * PIECE, :] = dq.reshape(PAIR, PIECE, HD)
        return 0

    lax.fori_loop(0, BLOCKS, one_block, 0)
    for column in range(REACH + 1):
        for piece in range(KVH):
            base = (REACH - column) * COL + piece * 2 * TOK
            for ref, which in ((mine_ref, core), (theirs_ref, 1 - core)):
                at = pl.ds(pl.multiple_of(base + which * TOK, TOK), TOK)
                ref[column, piece, 0:TOK] = (dk[at, :] * SCALE).astype(ref.dtype)
                ref[column, piece, TOK : 2 * TOK] = dv[at, :].astype(ref.dtype)


def old_terms(mine_ref, got_ref, one_ref, two_ref):
    one_ref[...] = (mine_ref[1] + got_ref[1].astype(F32)).astype(BF16)
    two_ref[...] = (mine_ref[2] + got_ref[2].astype(F32)).astype(BF16)


def add_terms(mine_ref, got_ref, one_ref, two_ref, out_ref):
    out_ref[...] = (
        mine_ref[0] + got_ref[0].astype(F32) + one_ref[...].astype(F32) + two_ref[...].astype(F32)
    ).astype(BF16)


def exchange(x):
    return lax.all_to_all(x, RING, split_axis=0, concat_axis=0, tiled=True)


def shifted(x, by):
    count = SIZES[0] * SIZES[1]
    return lax.ppermute(x, COLUMNS, [(i, (i + by) % count) for i in range(count)])


def swapped(x):
    return lax.ppermute(x, "c", [(0, 1), (1, 0)])


def starts(doc_lengths, column, core):
    ends = jnp.cumsum(doc_lengths)
    row = jnp.arange(ROWS, dtype=jnp.int32)
    piece = jnp.arange(BLOCKS, dtype=jnp.int32)[:, None] * PAIR + (row // PIECE)[None, :]
    place = column * COL + piece * (2 * TOK) + core * TOK + ((row % PIECE) // GROUP)[None, :]
    start = jnp.max(jnp.where(ends[:, None, None] <= place[None], ends[:, None, None], 0), axis=0)
    return jnp.maximum(start - (column - REACH) * COL, 0).astype(jnp.int32)[:, None, :]


def shards(query_in, key_in, value_in, grad_out, doc_lengths):
    both_kv = shape(KVH, 2 * TOK, HD)
    both_wide = shape(KVH, 2 * PIECE, HD)
    heads_kv = shape(TOK, KVH, HD)
    heads_wide = shape(TOK, KVH * GROUP, HD)
    wide = [pltpu.VMEM((TOK * KVH, HD), F32)]

    kv = exchange(call(pack_kv, [both_kv], [VMEM] * 2, wide, "pack_kv")(key_in, value_in)[0])
    qg = exchange(call(pack_qg, [both_wide], [VMEM] * 2, [], "pack_qg")(query_in, grad_out)[0])
    other = swapped(kv)
    old = jnp.stack([shifted(kv, 1), shifted(kv, 2)])
    other_old = swapped(old)

    core = lax.axis_index("c").astype(jnp.int32)
    start = starts(doc_lengths, lax.axis_index(COLUMNS), core)
    od, mine, theirs = call(
        attend,
        [both_wide, shape(REACH + 1, KVH, 2 * TOK, HD, dtype=F32), shape(REACH + 1, KVH, 2 * TOK, HD)],
        [SMEM] + [VMEM] * 6,
        [pltpu.VMEM((KEYS, HD), BF16)] * 2
        + [pltpu.VMEM((HD, KEYS), BF16)] * 2
        + [pltpu.VMEM((WIN * TILE, ROWS), F32)]
        + [pltpu.VMEM((WIN * TILE, ROWS), BF16)] * 2
        + [pltpu.VMEM((KEYS, HD), F32)] * 2,
        "attend",
        12 * BLOCKS * ROWS * WIN * TILE * HD,
    )(core[None], qg, start, kv, other, old, other_old)

    od_back = exchange(od)
    got = swapped(theirs)
    one, two = call(old_terms, [both_kv] * 2, [VMEM] * 2, [], "old_terms")(mine, got)
    one, two = shifted(one, -1), shifted(two, -2)
    total = call(add_terms, [both_kv], [VMEM] * 4, [], "add_terms")(mine, got, one, two)[0]
    od_back, total = lax.optimization_barrier((od_back, total))
    grads_kv = exchange(total)
    attn_out, grad_query = call(unpack_od, [heads_wide] * 2, [VMEM], [], "unpack_od")(od_back)
    grad_key, grad_value = call(unpack_kv, [heads_kv] * 2, [VMEM], wide, "unpack_kv")(grads_kv)
    return (attn_out, grad_query, grad_key, grad_value)


def solution(mesh):
    fine = Mesh(mesh.devices.reshape(SIZES), AXES)
    tokens = P(AXES, None, None)
    return jax.shard_map(
        shards,
        mesh=fine,
        in_specs=(tokens, tokens, tokens, tokens, P()),
        out_specs=(tokens, tokens, tokens, tokens),
        check_vma=False,
    )
```

```python
import math

import jax
import jax.numpy as jnp
from jax import lax
from jax.experimental import pallas as pl
from jax.experimental.pallas import tpu as pltpu
from jax.sharding import Mesh
from jax.sharding import PartitionSpec as P

AXES = ("x", "y", "l", "h", "c")
SIZES = (4, 8, 2, 4, 2)
RING = ("l", "h")
COLUMNS = ("x", "y")

HD = 128
KVH = 8
GROUP = 8
TOK = 32
COL = 512
REACH = 2
KEYS = (REACH + 1) * COL
PIECE = TOK * GROUP
TILE = 128
PAIR = 2
ROWS = PAIR * PIECE
BLOCKS = KVH // PAIR
WIN = 9
SCALE = HD**-0.5
SCALE2 = SCALE * math.log2(math.e)
NEG = -1e30

F32 = jnp.float32
BF16 = jnp.bfloat16
VMEM = pl.BlockSpec(memory_space=pltpu.VMEM)
SMEM = pl.BlockSpec(memory_space=pltpu.SMEM)
NT = (((1,), (1,)), ((), ()))
NN = (((1,), (0,)), ((), ()))


def dot(a, b, dims):
    return lax.dot_general(a, b, dims, preferred_element_type=F32)


def call(kernel, outs, ins, scratch, name, flops=0, nbytes=1 << 20):
    return pl.pallas_call(
        kernel,
        out_shape=outs,
        in_specs=ins,
        out_specs=[VMEM] * len(outs),
        scratch_shapes=scratch,
        compiler_params=pltpu.CompilerParams(vmem_limit_bytes=48 << 20),
        cost_estimate=pl.CostEstimate(flops=flops, bytes_accessed=nbytes, transcendentals=0),
        name=name,
    )


def shape(*dims, dtype=BF16):
    return jax.ShapeDtypeStruct(dims, dtype)


def put_heads(x_ref, out_ref, at):
    for pair in range(KVH // 2):
        both = x_ref[:, pair * 2 * GROUP : (pair + 1) * 2 * GROUP, :].astype(F32)
        for part in range(2):
            half = both[:, part * GROUP : (part + 1) * GROUP, :]
            out_ref[2 * pair + part, at : at + PIECE, :] = half.reshape(PIECE, HD).astype(BF16)


def take_heads(x_ref, at, out_ref):
    for pair in range(KVH // 2):
        halves = [
            x_ref[2 * pair + part, at : at + PIECE, :].astype(F32).reshape(TOK, GROUP, HD)
            for part in range(2)
        ]
        both = jnp.concatenate(halves, axis=1).astype(BF16)
        out_ref[:, pair * 2 * GROUP : (pair + 1) * 2 * GROUP, :] = both


def pack_kv(k_ref, v_ref, out_ref, wide):
    for at, ref in ((0, k_ref), (TOK, v_ref)):
        wide[...] = ref[...].astype(F32).reshape(TOK * KVH, HD)
        for j in range(KVH):
            out_ref[j, at : at + TOK, :] = wide[pl.ds(j, TOK, stride=KVH), :].astype(BF16)


def pack_qg(q_ref, g_ref, out_ref):
    put_heads(q_ref, out_ref, 0)
    put_heads(g_ref, out_ref, PIECE)


def unpack_od(x_ref, out_ref, dq_ref):
    take_heads(x_ref, 0, out_ref)
    take_heads(x_ref, PIECE, dq_ref)


def unpack_kv(x_ref, k_ref, v_ref, wide):
    for at, ref in ((0, k_ref), (TOK, v_ref)):
        for j in range(KVH):
            wide[pl.ds(j, TOK, stride=KVH), :] = x_ref[j, at : at + TOK, :].astype(F32)
        ref[...] = wide[...].reshape(TOK, KVH, HD).astype(BF16)


def attend(core_ref, qg_ref, start_ref, own_ref, other_ref, old_ref, other_old_ref,
           od_ref, mine_ref, theirs_ref,
           keys, values, keys_t, values_t, scores, probs, dscores, dk, dv):
    core = core_ref[0]
    for column in range(REACH + 1):
        for piece in range(KVH):
            base = (REACH - column) * COL + piece * 2 * TOK
            for ref, old, which in ((own_ref, old_ref, core), (other_ref, other_old_ref, 1 - core)):
                at = pl.ds(pl.multiple_of(base + which * TOK, TOK), TOK)
                got = ref[piece] if column == 0 else old[column - 1, piece]
                keys[at, :] = got[0:TOK]
                values[at, :] = got[TOK : 2 * TOK]
    for t in range(KEYS // TILE):
        at = slice(t * TILE, (t + 1) * TILE)
        keys_t[:, at] = jnp.transpose(keys[at, :])
        values_t[:, at] = jnp.transpose(values[at, :])
    dk[...] = jnp.zeros(dk.shape, F32)
    dv[...] = jnp.zeros(dv.shape, F32)
    index = lax.broadcasted_iota(jnp.int32, (TILE, ROWS), 0)
    row = lax.broadcasted_iota(jnp.int32, (1, ROWS), 1)
    inside = (row // PIECE) * (2 * TOK) + core * TOK + (row % PIECE) // GROUP

    tiles = [slice(t * TILE, (t + 1) * TILE) for t in range(WIN)]

    class Block:
        def __init__(self, at):
            self.slot = at % 2
            self.base = at * TILE
            self.window = slice(self.base, self.base + WIN * TILE)
            self.pieces = slice(at * PAIR, (at + 1) * PAIR)
            self.q = qg_ref[self.pieces, 0:PIECE, :].reshape(ROWS, HD)
            self.g = qg_ref[self.pieces, PIECE : 2 * PIECE, :].reshape(ROWS, HD)
            self.g_t = jnp.transpose(self.g.astype(F32))
            self.start = start_ref[at] - self.base
            self.top = jnp.full((8, ROWS), NEG, F32)
            self.sums = jnp.zeros((8, ROWS), F32)

        def keys_of(self, t):
            return slice(self.base + t * TILE, self.base + (t + 1) * TILE)

        def score(self, t):
            s = dot(keys[self.keys_of(t), :], self.q, NT)
            seen = index >= self.start - t * TILE
            if t == WIN - 1:
                seen = seen & (index <= inside)
            s = jnp.where(seen, s, NEG)
            scores[tiles[t], :] = s
            self.top = jnp.maximum(self.top, jnp.max(s.reshape(TILE // 8, 8, ROWS), axis=0))

        def find_top(self):
            self.row_top = jnp.max(self.top, axis=0, keepdims=True) * SCALE2

        def weigh(self, t):
            p = jnp.exp2(scores[tiles[t], :] * SCALE2 - self.row_top)
            self.sums = self.sums + jnp.sum(p.reshape(TILE // 8, 8, ROWS), axis=0)
            probs[self.slot, tiles[t], :] = p.astype(BF16)

        def output(self):
            self.inv = 1.0 / jnp.sum(self.sums, axis=0, keepdims=True)
            out = dot(values_t[:, self.window], probs[self.slot], NN) * self.inv
            self.drift = jnp.sum(out * self.g_t, axis=0, keepdims=True)
            od_ref[self.pieces, 0:PIECE, :] = jnp.transpose(out).astype(BF16).reshape(PAIR, PIECE, HD)
            inv = jnp.transpose(jnp.broadcast_to(self.inv, (8, ROWS)))[:, 0:1]
            self.g_scaled = (self.g.astype(F32) * inv).astype(BF16)
            self.q_scaled = (self.q.astype(F32) * inv).astype(BF16)

        def dscore(self, t):
            dp = dot(values[self.keys_of(t), :], self.g, NT)
            dscores[self.slot, tiles[t], :] = (dp - self.drift).astype(BF16) * probs[self.slot, tiles[t], :]

        def key_terms(self, t):
            at = self.keys_of(t)
            dv[at, :] += dot(probs[self.slot, tiles[t], :], self.g_scaled, NN)
            dk[at, :] += dot(dscores[self.slot, tiles[t], :], self.q_scaled, NN)

        def dquery(self):
            dq = dot(keys_t[:, self.window], dscores[self.slot], NN) * (self.inv * SCALE)
            od_ref[self.pieces, PIECE : 2 * PIECE, :] = jnp.transpose(dq).astype(BF16).reshape(PAIR, PIECE, HD)

    last = None
    for at in range(BLOCKS + 1):
        block = Block(at) if at < BLOCKS else None
        for t in range(WIN):
            if block:
                block.score(t)
            if last:
                last.dscore(t)
        if block:
            block.find_top()
        for t in range(WIN):
            if block:
                block.weigh(t)
            if last:
                last.key_terms(t)
        if last:
            last.dquery()
        if block:
            block.output()
        last = block

    for column in range(REACH + 1):
        for piece in range(KVH):
            base = (REACH - column) * COL + piece * 2 * TOK
            for ref, which in ((mine_ref, core), (theirs_ref, 1 - core)):
                at = pl.ds(pl.multiple_of(base + which * TOK, TOK), TOK)
                ref[column, piece, 0:TOK] = (dk[at, :] * SCALE).astype(ref.dtype)
                ref[column, piece, TOK : 2 * TOK] = dv[at, :].astype(ref.dtype)


def old_terms(mine_ref, got_ref, one_ref, two_ref):
    one_ref[...] = (mine_ref[1] + got_ref[1].astype(F32)).astype(BF16)
    two_ref[...] = (mine_ref[2] + got_ref[2].astype(F32)).astype(BF16)


def add_terms(mine_ref, got_ref, one_ref, two_ref, out_ref):
    out_ref[...] = (
        mine_ref[0] + got_ref[0].astype(F32) + one_ref[...].astype(F32) + two_ref[...].astype(F32)
    ).astype(BF16)


def exchange(x):
    return lax.all_to_all(x, RING, split_axis=0, concat_axis=0, tiled=True)


def shifted(x, by):
    count = SIZES[0] * SIZES[1]
    return lax.ppermute(x, COLUMNS, [(i, (i + by) % count) for i in range(count)])


def swapped(x):
    return lax.ppermute(x, "c", [(0, 1), (1, 0)])


def starts(doc_lengths, column, core):
    ends = jnp.cumsum(doc_lengths)
    row = jnp.arange(ROWS, dtype=jnp.int32)
    piece = jnp.arange(BLOCKS, dtype=jnp.int32)[:, None] * PAIR + (row // PIECE)[None, :]
    place = column * COL + piece * (2 * TOK) + core * TOK + ((row % PIECE) // GROUP)[None, :]
    start = jnp.max(jnp.where(ends[:, None, None] <= place[None], ends[:, None, None], 0), axis=0)
    return jnp.maximum(start - (column - REACH) * COL, 0).astype(jnp.int32)[:, None, :]


def shards(query_in, key_in, value_in, grad_out, doc_lengths):
    both_kv = shape(KVH, 2 * TOK, HD)
    both_wide = shape(KVH, 2 * PIECE, HD)
    heads_kv = shape(TOK, KVH, HD)
    heads_wide = shape(TOK, KVH * GROUP, HD)
    wide = [pltpu.VMEM((TOK * KVH, HD), F32)]

    kv = exchange(call(pack_kv, [both_kv], [VMEM] * 2, wide, "pack_kv")(key_in, value_in)[0])
    qg = exchange(call(pack_qg, [both_wide], [VMEM] * 2, [], "pack_qg")(query_in, grad_out)[0])
    other = swapped(kv)
    old = jnp.stack([shifted(kv, 1), shifted(kv, 2)])
    other_old = swapped(old)

    core = lax.axis_index("c").astype(jnp.int32)
    start = starts(doc_lengths, lax.axis_index(COLUMNS), core)
    od, mine, theirs = call(
        attend,
        [both_wide, shape(REACH + 1, KVH, 2 * TOK, HD, dtype=F32), shape(REACH + 1, KVH, 2 * TOK, HD)],
        [SMEM] + [VMEM] * 6,
        [pltpu.VMEM((KEYS, HD), BF16)] * 2
        + [pltpu.VMEM((HD, KEYS), BF16)] * 2
        + [pltpu.VMEM((WIN * TILE, ROWS), F32)]
        + [pltpu.VMEM((2, WIN * TILE, ROWS), BF16)] * 2
        + [pltpu.VMEM((KEYS, HD), F32)] * 2,
        "attend",
        12 * BLOCKS * ROWS * WIN * TILE * HD,
    )(core[None], qg, start, kv, other, old, other_old)

    od_back = exchange(od)
    got = swapped(theirs)
    one, two = call(old_terms, [both_kv] * 2, [VMEM] * 2, [], "old_terms")(mine, got)
    one, two = shifted(one, -1), shifted(two, -2)
    total = call(add_terms, [both_kv], [VMEM] * 4, [], "add_terms")(mine, got, one, two)[0]
    od_back, total = lax.optimization_barrier((od_back, total))
    grads_kv = exchange(total)
    attn_out, grad_query = call(unpack_od, [heads_wide] * 2, [VMEM], [], "unpack_od")(od_back)
    grad_key, grad_value = call(unpack_kv, [heads_kv] * 2, [VMEM], wide, "unpack_kv")(grads_kv)
    return (attn_out, grad_query, grad_key, grad_value)


def solution(mesh):
    fine = Mesh(mesh.devices.reshape(SIZES), AXES)
    tokens = P(AXES, None, None)
    return jax.shard_map(
        shards,
        mesh=fine,
        in_specs=(tokens, tokens, tokens, tokens, P()),
        out_specs=(tokens, tokens, tokens, tokens),
        check_vma=False,
    )
```

```python
import math

import jax
import jax.numpy as jnp
from jax import lax
from jax.experimental import pallas as pl
from jax.experimental.pallas import tpu as pltpu
from jax.sharding import Mesh
from jax.sharding import PartitionSpec as P

AXES = ("x", "y", "l", "h", "k", "c")
SIZES = (4, 8, 2, 2, 2, 2)
RING = ("l", "h", "k")
COLUMNS = ("x", "y")

HD = 128
KVH = 8
GROUP = 8
TOK = 32
COL = 512
REACH = 2
KEYS = (REACH + 1) * COL
PIECE = TOK * GROUP
TILE = 128
PAIR = 2
ROWS = PAIR * PIECE
BLOCKS = KVH // PAIR
PLACES = [
    sum((p >> ("k", "h", "l").index(axis) & 1) << (2 - n) for n, axis in enumerate(RING)) for p in range(KVH)
]
WIN = 9
NEAR = WIN - BLOCKS
SCALE = HD**-0.5
SCALE2 = SCALE * math.log2(math.e)
NEG = -1e30

F32 = jnp.float32
BF16 = jnp.bfloat16
VMEM = pl.BlockSpec(memory_space=pltpu.VMEM)
SMEM = pl.BlockSpec(memory_space=pltpu.SMEM)
NT = (((1,), (1,)), ((), ()))
NN = (((1,), (0,)), ((), ()))


def dot(a, b, dims):
    return lax.dot_general(a, b, dims, preferred_element_type=F32)


def call(kernel, outs, ins, scratch, name, flops=0, nbytes=1 << 20):
    return pl.pallas_call(
        kernel,
        out_shape=outs,
        in_specs=ins,
        out_specs=[VMEM] * len(outs),
        scratch_shapes=scratch,
        compiler_params=pltpu.CompilerParams(vmem_limit_bytes=48 << 20),
        cost_estimate=pl.CostEstimate(flops=flops, bytes_accessed=nbytes, transcendentals=0),
        name=name,
    )


def shape(*dims, dtype=BF16):
    return jax.ShapeDtypeStruct(dims, dtype)


def put_heads(x_ref, out_ref, at):
    for pair in range(KVH // 2):
        both = x_ref[:, pair * 2 * GROUP : (pair + 1) * 2 * GROUP, :].astype(F32)
        for part in range(2):
            half = both[:, part * GROUP : (part + 1) * GROUP, :]
            out_ref[2 * pair + part, at : at + PIECE, :] = half.reshape(PIECE, HD).astype(BF16)


def take_heads(x_ref, at, out_ref):
    for pair in range(KVH // 2):
        halves = [
            x_ref[2 * pair + part, at : at + PIECE, :].astype(F32).reshape(TOK, GROUP, HD)
            for part in range(2)
        ]
        both = jnp.concatenate(halves, axis=1).astype(BF16)
        out_ref[:, pair * 2 * GROUP : (pair + 1) * 2 * GROUP, :] = both


def pack_qg(q_ref, g_ref, out_ref):
    put_heads(q_ref, out_ref, 0)
    put_heads(g_ref, out_ref, PIECE)


def unpack_od(x_ref, out_ref, dq_ref):
    take_heads(x_ref, 0, out_ref)
    take_heads(x_ref, PIECE, dq_ref)


def unpack_kv(x_ref, k_ref, v_ref, wide):
    for at, ref in ((0, k_ref), (TOK, v_ref)):
        for j in range(KVH):
            wide[pl.ds(j, TOK, stride=KVH), :] = x_ref[j, at : at + TOK, :].astype(F32)
        ref[...] = wide[...].reshape(TOK, KVH, HD).astype(BF16)


def attend(where_ref, qg_ref, start_ref, own_ref, other_ref, old_ref, other_old_ref,
           od_ref, mine_ref, theirs_ref,
           keys, values, keys_t, values_t, scores, probs, dscores, dk, dv):
    core = where_ref[0]
    for column in range(REACH + 1):
        for piece in range(KVH):
            base = (REACH - column) * COL + piece * 2 * TOK
            for ref, old, which in ((own_ref, old_ref, core), (other_ref, other_old_ref, 1 - core)):
                at = pl.ds(pl.multiple_of(base + which * TOK, TOK), TOK)
                got = ref[PLACES[piece]] if column == 0 else old[column - 1, PLACES[piece]]
                keys[at, :] = got[0:TOK]
                values[at, :] = got[TOK : 2 * TOK]
    for t in range(KEYS // TILE):
        at = slice(t * TILE, (t + 1) * TILE)
        keys_t[:, at] = jnp.transpose(keys[at, :])
        values_t[:, at] = jnp.transpose(values[at, :])
    dk[...] = jnp.zeros(dk.shape, F32)
    dv[...] = jnp.zeros(dv.shape, F32)
    index = lax.broadcasted_iota(jnp.int32, (TILE, ROWS), 0)
    row = lax.broadcasted_iota(jnp.int32, (1, ROWS), 1)
    inside = (row // PIECE) * (2 * TOK) + core * TOK + (row % PIECE) // GROUP

    tiles = [slice(t * TILE, (t + 1) * TILE) for t in range(WIN)]

    class Block:
        def __init__(self, at, count):
            self.slot = at % 2
            self.count = count
            self.base = (at + WIN - count) * TILE
            self.window = slice(self.base, self.base + count * TILE)
            self.held = slice(0, count * TILE)
            self.pieces = PLACES[at * PAIR : (at + 1) * PAIR]
            self.q = jnp.concatenate([qg_ref[p, 0:PIECE, :] for p in self.pieces], axis=0)
            self.g = jnp.concatenate([qg_ref[p, PIECE : 2 * PIECE, :] for p in self.pieces], axis=0)
            self.g_t = jnp.transpose(self.g.astype(F32))
            self.start = start_ref[at] - self.base
            self.top = jnp.full((8, ROWS), NEG, F32)
            self.sums = jnp.zeros((8, ROWS), F32)

        def keys_of(self, t):
            return slice(self.base + t * TILE, self.base + (t + 1) * TILE)

        def put(self, at, result):
            rows = jnp.transpose(result).astype(BF16)
            for n, p in enumerate(self.pieces):
                od_ref[p, at : at + PIECE, :] = rows[n * PIECE : (n + 1) * PIECE]

        def score(self, t):
            s = dot(keys[self.keys_of(t), :], self.q, NT)
            seen = index >= self.start - t * TILE
            if t == self.count - 1:
                seen = seen & (index <= inside)
            s = jnp.where(seen, s, NEG)
            scores[tiles[t], :] = s
            self.top = jnp.maximum(self.top, jnp.max(s.reshape(TILE // 8, 8, ROWS), axis=0))

        def find_top(self):
            self.row_top = jnp.max(self.top, axis=0, keepdims=True) * SCALE2

        def weigh(self, t):
            p = jnp.exp2(scores[tiles[t], :] * SCALE2 - self.row_top)
            self.sums = self.sums + jnp.sum(p.reshape(TILE // 8, 8, ROWS), axis=0)
            probs[self.slot, tiles[t], :] = p.astype(BF16)

        def output(self):
            self.inv = 1.0 / jnp.sum(self.sums, axis=0, keepdims=True)
            out = dot(values_t[:, self.window], probs[self.slot, self.held], NN) * self.inv
            self.drift = jnp.sum(out * self.g_t, axis=0, keepdims=True)
            self.put(0, out)
            self.g_scaled = jnp.transpose((self.g_t * self.inv).astype(BF16))

        def dscore(self, t):
            dp = dot(values[self.keys_of(t), :], self.g, NT)
            ds = ((dp - self.drift) * self.inv).astype(BF16)
            dscores[self.slot, tiles[t], :] = ds * probs[self.slot, tiles[t], :]

        def dvalue(self):
            dv[self.window, :] += dot(probs[self.slot, self.held], self.g_scaled, NN)

        def dkey(self):
            dk[self.window, :] += dot(dscores[self.slot, self.held], self.q, NN)

        def dquery(self):
            self.put(PIECE, dot(keys_t[:, self.window], dscores[self.slot, self.held], NN) * SCALE)

    def pipeline(counts):
        last = None
        for at in range(BLOCKS + 1):
            block = Block(at, counts[at]) if at < BLOCKS else None
            for t in range(WIN):
                if block and t < block.count:
                    block.score(t)
                if last and t < last.count:
                    last.dscore(t)
            if block:
                block.find_top()
            if last:
                last.dvalue()
            for t in range(WIN):
                if block and t < block.count:
                    block.weigh(t)
            if last:
                last.dkey()
                last.dquery()
            if block:
                block.output()
            last = block

    @pl.when(where_ref[1] == 0)
    def near():
        pipeline([NEAR + 1 + at for at in range(BLOCKS)])

    @pl.when(where_ref[1] != 0)
    def far():
        pipeline([WIN] * (BLOCKS - 1) + [BLOCKS])

    for column in range(REACH + 1):
        for piece in range(KVH):
            base = (REACH - column) * COL + piece * 2 * TOK
            for ref, which in ((mine_ref, core), (theirs_ref, 1 - core)):
                at = pl.ds(pl.multiple_of(base + which * TOK, TOK), TOK)
                ref[column, PLACES[piece], 0:TOK] = (dk[at, :] * SCALE).astype(ref.dtype)
                ref[column, PLACES[piece], TOK : 2 * TOK] = dv[at, :].astype(ref.dtype)


def old_terms(mine_ref, got_ref, one_ref, two_ref):
    one_ref[...] = (mine_ref[1] + got_ref[1].astype(F32)).astype(BF16)
    two_ref[...] = (mine_ref[2] + got_ref[2].astype(F32)).astype(BF16)


def add_terms(mine_ref, got_ref, one_ref, two_ref, out_ref):
    out_ref[...] = (
        mine_ref[0] + got_ref[0].astype(F32) + one_ref[...].astype(F32) + two_ref[...].astype(F32)
    ).astype(BF16)


def exchange(x):
    return lax.all_to_all(x, RING, split_axis=0, concat_axis=0, tiled=True)


def shifted(x, by):
    count = SIZES[0] * SIZES[1]
    return lax.ppermute(x, COLUMNS, [(i, (i + by) % count) for i in range(count)])


def swapped(x):
    return lax.ppermute(x, "c", [(0, 1), (1, 0)])


def starts(doc_lengths, column, core):
    ends = jnp.cumsum(doc_lengths)
    row = jnp.arange(ROWS, dtype=jnp.int32)
    piece = jnp.arange(BLOCKS, dtype=jnp.int32)[:, None] * PAIR + (row // PIECE)[None, :]
    place = column * COL + piece * (2 * TOK) + core * TOK + ((row % PIECE) // GROUP)[None, :]
    start = jnp.max(jnp.where(ends[:, None, None] <= place[None], ends[:, None, None], 0), axis=0)
    return jnp.maximum(start - (column - REACH) * COL, 0).astype(jnp.int32)[:, None, :]


def shards(query_in, key_in, value_in, grad_out, doc_lengths):
    both_kv = shape(KVH, 2 * TOK, HD)
    both_wide = shape(KVH, 2 * PIECE, HD)
    heads_kv = shape(TOK, KVH, HD)
    heads_wide = shape(TOK, KVH * GROUP, HD)
    wide = [pltpu.VMEM((TOK * KVH, HD), F32)]

    packed = jnp.transpose(jnp.stack([key_in, value_in]), (2, 0, 1, 3)).reshape(KVH, 2 * TOK, HD)
    kv = exchange(packed)
    qg = exchange(call(pack_qg, [both_wide], [VMEM] * 2, [], "pack_qg")(query_in, grad_out)[0])
    other = swapped(kv)
    old = jnp.stack([shifted(kv, 1), shifted(kv, 2)])
    old, other = lax.optimization_barrier((old, other))
    other_old = swapped(old)

    core = lax.axis_index("c").astype(jnp.int32)
    start = starts(doc_lengths, lax.axis_index(COLUMNS), core)
    where = jnp.stack([core, (start[0, 0, 0] < REACH * COL - NEAR * TILE).astype(jnp.int32)])
    od, mine, theirs = call(
        attend,
        [both_wide, shape(REACH + 1, KVH, 2 * TOK, HD, dtype=F32), shape(REACH + 1, KVH, 2 * TOK, HD)],
        [SMEM] + [VMEM] * 6,
        [pltpu.VMEM((KEYS, HD), BF16)] * 2
        + [pltpu.VMEM((HD, KEYS), BF16)] * 2
        + [pltpu.VMEM((WIN * TILE, ROWS), F32)]
        + [pltpu.VMEM((2, WIN * TILE, ROWS), BF16)] * 2
        + [pltpu.VMEM((KEYS, HD), F32)] * 2,
        "attend",
        12 * BLOCKS * ROWS * WIN * TILE * HD,
    )(where, qg, start, kv, other, old, other_old)

    od_back = exchange(od)
    got = swapped(theirs)
    one, two = call(old_terms, [both_kv] * 2, [VMEM] * 2, [], "old_terms")(mine, got)
    one, two = shifted(one, -1), shifted(two, -2)
    total = call(add_terms, [both_kv], [VMEM] * 4, [], "add_terms")(mine, got, one, two)[0]
    od_back, total = lax.optimization_barrier((od_back, total))
    grads_kv = exchange(total)
    attn_out, grad_query = call(unpack_od, [heads_wide] * 2, [VMEM], [], "unpack_od")(od_back)
    grad_key, grad_value = call(unpack_kv, [heads_kv] * 2, [VMEM], wide, "unpack_kv")(grads_kv)
    return (attn_out, grad_query, grad_key, grad_value)


def solution(mesh):
    fine = Mesh(mesh.devices.reshape(SIZES), AXES)
    tokens = P(AXES, None, None)
    return jax.shard_map(
        shards,
        mesh=fine,
        in_specs=(tokens, tokens, tokens, tokens, P()),
        out_specs=(tokens, tokens, tokens, tokens),
        check_vma=False,
    )
```

```python
import math

import jax
import jax.numpy as jnp
from jax import lax
from jax.experimental import pallas as pl
from jax.experimental.pallas import tpu as pltpu
from jax.sharding import Mesh
from jax.sharding import PartitionSpec as P

AXES = ("x", "y", "l", "h", "k", "c")
SIZES = (4, 8, 2, 2, 2, 2)
RING = ("l", "h", "k")
COLUMNS = ("x", "y")

HD = 128
KVH = 8
GROUP = 8
TOK = 32
COL = 512
REACH = 2
KEYS = (REACH + 1) * COL
PIECE = TOK * GROUP
TILE = 128
PAIR = 2
ROWS = PAIR * PIECE
BLOCKS = KVH // PAIR
PLACES = [
    sum((p >> ("k", "h", "l").index(axis) & 1) << (2 - n) for n, axis in enumerate(RING)) for p in range(KVH)
]
WIN = 9
NEAR = WIN - BLOCKS
SCALE = HD**-0.5
SCALE2 = SCALE * math.log2(math.e)
NEG = -1e30

F32 = jnp.float32
BF16 = jnp.bfloat16
VMEM = pl.BlockSpec(memory_space=pltpu.VMEM)
SMEM = pl.BlockSpec(memory_space=pltpu.SMEM)
HBM = pl.BlockSpec(memory_space=pl.ANY)
NT = (((1,), (1,)), ((), ()))
NN = (((1,), (0,)), ((), ()))


def dot(a, b, dims):
    return lax.dot_general(a, b, dims, preferred_element_type=F32)


def call(kernel, outs, ins, scratch, name, flops=0, nbytes=1 << 20, first=VMEM):
    return pl.pallas_call(
        kernel,
        out_shape=outs,
        in_specs=ins,
        out_specs=[first] + [VMEM] * (len(outs) - 1),
        scratch_shapes=scratch,
        compiler_params=pltpu.CompilerParams(vmem_limit_bytes=48 << 20),
        cost_estimate=pl.CostEstimate(flops=flops, bytes_accessed=nbytes, transcendentals=0),
        name=name,
    )


def shape(*dims, dtype=BF16):
    return jax.ShapeDtypeStruct(dims, dtype)


def put_heads(x_ref, out_ref, at):
    for pair in range(KVH // 2):
        both = x_ref[:, pair * 2 * GROUP : (pair + 1) * 2 * GROUP, :].astype(F32)
        for part in range(2):
            half = both[:, part * GROUP : (part + 1) * GROUP, :]
            out_ref[2 * pair + part, at : at + PIECE, :] = half.reshape(PIECE, HD).astype(BF16)


def take_heads(x_ref, at, out_ref):
    for pair in range(KVH // 2):
        halves = [
            x_ref[2 * pair + part, at : at + PIECE, :].astype(F32).reshape(TOK, GROUP, HD)
            for part in range(2)
        ]
        both = jnp.concatenate(halves, axis=1).astype(BF16)
        out_ref[:, pair * 2 * GROUP : (pair + 1) * 2 * GROUP, :] = both


def pack_qg(q_ref, g_ref, out_ref):
    put_heads(q_ref, out_ref, 0)
    put_heads(g_ref, out_ref, PIECE)


def unpack_od(x_ref, out_ref, dq_ref):
    take_heads(x_ref, 0, out_ref)
    take_heads(x_ref, PIECE, dq_ref)


def unpack_kv(x_ref, k_ref, v_ref, wide):
    for at, ref in ((0, k_ref), (TOK, v_ref)):
        for j in range(KVH):
            wide[pl.ds(j, TOK, stride=KVH), :] = x_ref[j, at : at + TOK, :].astype(F32)
        ref[...] = wide[...].reshape(TOK, KVH, HD).astype(BF16)


def attend(where_ref, qg_ref, start_ref, own_ref, other_ref, old_ref, other_old_ref,
           od_ref, mine_ref, theirs_ref,
           keys, values, keys_t, values_t, scores, probs, dscores, dk, dv, od, sems):
    core = where_ref[0]
    for column in range(REACH + 1):
        for piece in range(KVH):
            base = (REACH - column) * COL + piece * 2 * TOK
            for ref, old, which in ((own_ref, old_ref, core), (other_ref, other_old_ref, 1 - core)):
                at = pl.ds(pl.multiple_of(base + which * TOK, TOK), TOK)
                got = ref[PLACES[piece]] if column == 0 else old[column - 1, PLACES[piece]]
                keys[at, :] = got[0:TOK]
                values[at, :] = got[TOK : 2 * TOK]
    for t in range(KEYS // TILE):
        at = slice(t * TILE, (t + 1) * TILE)
        keys_t[:, at] = jnp.transpose(keys[at, :])
        values_t[:, at] = jnp.transpose(values[at, :])
    dk[...] = jnp.zeros(dk.shape, F32)
    dv[...] = jnp.zeros(dv.shape, F32)
    index = lax.broadcasted_iota(jnp.int32, (TILE, ROWS), 0)
    row = lax.broadcasted_iota(jnp.int32, (1, ROWS), 1)
    inside = (row // PIECE) * (2 * TOK) + core * TOK + (row % PIECE) // GROUP

    tiles = [slice(t * TILE, (t + 1) * TILE) for t in range(WIN)]

    class Block:
        def __init__(self, at, count, sent):
            self.sent = sent
            self.slot = at % 2
            self.count = count
            self.base = (at + WIN - count) * TILE
            self.window = slice(self.base, self.base + count * TILE)
            self.held = slice(0, count * TILE)
            self.pieces = PLACES[at * PAIR : (at + 1) * PAIR]
            self.q = jnp.concatenate([qg_ref[p, 0:PIECE, :] for p in self.pieces], axis=0)
            self.g = jnp.concatenate([qg_ref[p, PIECE : 2 * PIECE, :] for p in self.pieces], axis=0)
            self.g_t = jnp.transpose(self.g.astype(F32))
            self.start = start_ref[at] - self.base
            self.top = jnp.full((8, ROWS), NEG, F32)
            self.sums = jnp.zeros((8, ROWS), F32)

        def keys_of(self, t):
            return slice(self.base + t * TILE, self.base + (t + 1) * TILE)

        def put(self, at, result):
            rows = jnp.transpose(result).astype(BF16)
            for n, p in enumerate(self.pieces):
                piece = (p, pl.ds(at, PIECE))
                od[piece] = rows[n * PIECE : (n + 1) * PIECE]
                copy = pltpu.make_async_copy(od.at[piece], od_ref.at[piece], sems.at[len(self.sent)])
                copy.start()
                self.sent.append(copy)

        def score(self, t):
            s = dot(keys[self.keys_of(t), :], self.q, NT)
            seen = index >= self.start - t * TILE
            if t == self.count - 1:
                seen = seen & (index <= inside)
            s = jnp.where(seen, s, NEG)
            scores[tiles[t], :] = s
            self.top = jnp.maximum(self.top, jnp.max(s.reshape(TILE // 8, 8, ROWS), axis=0))

        def find_top(self):
            self.row_top = jnp.max(self.top, axis=0, keepdims=True) * SCALE2

        def weigh(self, t):
            p = jnp.exp2(scores[tiles[t], :] * SCALE2 - self.row_top)
            self.sums = self.sums + jnp.sum(p.reshape(TILE // 8, 8, ROWS), axis=0)
            probs[self.slot, tiles[t], :] = p.astype(BF16)

        def output(self):
            self.inv = 1.0 / jnp.sum(self.sums, axis=0, keepdims=True)
            out = dot(values_t[:, self.window], probs[self.slot, self.held], NN) * self.inv
            self.drift = jnp.sum(out * self.g_t, axis=0, keepdims=True)
            self.put(0, out)
            self.g_scaled = jnp.transpose((self.g_t * self.inv).astype(BF16))

        def dscore(self, t):
            dp = dot(values[self.keys_of(t), :], self.g, NT)
            ds = ((dp - self.drift) * self.inv).astype(BF16)
            dscores[self.slot, tiles[t], :] = ds * probs[self.slot, tiles[t], :]

        def dvalue(self):
            dv[self.window, :] += dot(probs[self.slot, self.held], self.g_scaled, NN)

        def dkey(self):
            dk[self.window, :] += dot(dscores[self.slot, self.held], self.q, NN)

        def dquery(self):
            self.put(PIECE, dot(keys_t[:, self.window], dscores[self.slot, self.held], NN) * SCALE)

    def pipeline(counts):
        last = None
        sent = []
        for at in range(BLOCKS + 1):
            block = Block(at, counts[at], sent) if at < BLOCKS else None
            for t in range(WIN):
                if block and t < block.count:
                    block.score(t)
                if last and t < last.count:
                    last.dscore(t)
            if block:
                block.find_top()
            if last:
                last.dvalue()
            for t in range(WIN):
                if block and t < block.count:
                    block.weigh(t)
            if last:
                last.dkey()
                last.dquery()
            if block:
                block.output()
            last = block
        for copy in sent:
            copy.wait()

    @pl.when(where_ref[1] == 0)
    def near():
        pipeline([NEAR + 1 + at for at in range(BLOCKS)])

    @pl.when(where_ref[1] != 0)
    def far():
        pipeline([WIN] * (BLOCKS - 1) + [BLOCKS])

    for column in range(REACH + 1):
        for piece in range(KVH):
            base = (REACH - column) * COL + piece * 2 * TOK
            for ref, which in ((mine_ref, core), (theirs_ref, 1 - core)):
                at = pl.ds(pl.multiple_of(base + which * TOK, TOK), TOK)
                ref[column, PLACES[piece], 0:TOK] = (dk[at, :] * SCALE).astype(ref.dtype)
                ref[column, PLACES[piece], TOK : 2 * TOK] = dv[at, :].astype(ref.dtype)


def old_terms(mine_ref, got_ref, one_ref, two_ref):
    one_ref[...] = (mine_ref[1] + got_ref[1].astype(F32)).astype(BF16)
    two_ref[...] = (mine_ref[2] + got_ref[2].astype(F32)).astype(BF16)


def add_terms(mine_ref, got_ref, one_ref, two_ref, out_ref):
    out_ref[...] = (
        mine_ref[0] + got_ref[0].astype(F32) + one_ref[...].astype(F32) + two_ref[...].astype(F32)
    ).astype(BF16)


def exchange(x):
    return lax.all_to_all(x, RING, split_axis=0, concat_axis=0, tiled=True)


def shifted(x, by):
    count = SIZES[0] * SIZES[1]
    return lax.ppermute(x, COLUMNS, [(i, (i + by) % count) for i in range(count)])


def swapped(x):
    return lax.ppermute(x, "c", [(0, 1), (1, 0)])


def starts(doc_lengths, column, core):
    ends = jnp.cumsum(doc_lengths)
    row = jnp.arange(ROWS, dtype=jnp.int32)
    piece = jnp.arange(BLOCKS, dtype=jnp.int32)[:, None] * PAIR + (row // PIECE)[None, :]
    place = column * COL + piece * (2 * TOK) + core * TOK + ((row % PIECE) // GROUP)[None, :]
    start = jnp.max(jnp.where(ends[:, None, None] <= place[None], ends[:, None, None], 0), axis=0)
    return jnp.maximum(start - (column - REACH) * COL, 0).astype(jnp.int32)[:, None, :]


def shards(query_in, key_in, value_in, grad_out, doc_lengths):
    both_kv = shape(KVH, 2 * TOK, HD)
    both_wide = shape(KVH, 2 * PIECE, HD)
    heads_kv = shape(TOK, KVH, HD)
    heads_wide = shape(TOK, KVH * GROUP, HD)
    wide = [pltpu.VMEM((TOK * KVH, HD), F32)]

    packed = jnp.transpose(jnp.stack([key_in, value_in]), (2, 0, 1, 3)).reshape(KVH, 2 * TOK, HD)
    kv = exchange(packed)
    qg = exchange(call(pack_qg, [both_wide], [VMEM] * 2, [], "pack_qg")(query_in, grad_out)[0])
    other = swapped(kv)
    old = jnp.stack([shifted(kv, 1), shifted(kv, 2)])
    old, other = lax.optimization_barrier((old, other))
    other_old = swapped(old)

    core = lax.axis_index("c").astype(jnp.int32)
    start = starts(doc_lengths, lax.axis_index(COLUMNS), core)
    where = jnp.stack([core, (start[0, 0, 0] < REACH * COL - NEAR * TILE).astype(jnp.int32)])
    od, mine, theirs = call(
        attend,
        [both_wide, shape(REACH + 1, KVH, 2 * TOK, HD, dtype=F32), shape(REACH + 1, KVH, 2 * TOK, HD)],
        [SMEM] + [VMEM] * 6,
        [pltpu.VMEM((KEYS, HD), BF16)] * 2
        + [pltpu.VMEM((HD, KEYS), BF16)] * 2
        + [pltpu.VMEM((WIN * TILE, ROWS), F32)]
        + [pltpu.VMEM((2, WIN * TILE, ROWS), BF16)] * 2
        + [pltpu.VMEM((KEYS, HD), F32)] * 2
        + [pltpu.VMEM((KVH, 2 * PIECE, HD), BF16), pltpu.SemaphoreType.DMA((4 * BLOCKS,))],
        "attend",
        12 * BLOCKS * ROWS * WIN * TILE * HD,
        first=HBM,
    )(where, qg, start, kv, other, old, other_old)

    od_back = exchange(od)
    got = swapped(theirs)
    one, two = call(old_terms, [both_kv] * 2, [VMEM] * 2, [], "old_terms")(mine, got)
    one, two = shifted(one, -1), shifted(two, -2)
    total = call(add_terms, [both_kv], [VMEM] * 4, [], "add_terms")(mine, got, one, two)[0]
    od_back, total = lax.optimization_barrier((od_back, total))
    grads_kv = exchange(total)
    attn_out, grad_query = call(unpack_od, [heads_wide] * 2, [VMEM], [], "unpack_od")(od_back)
    grad_key, grad_value = call(unpack_kv, [heads_kv] * 2, [VMEM], wide, "unpack_kv")(grads_kv)
    return (attn_out, grad_query, grad_key, grad_value)


def solution(mesh):
    fine = Mesh(mesh.devices.reshape(SIZES), AXES)
    tokens = P(AXES, None, None)
    return jax.shard_map(
        shards,
        mesh=fine,
        in_specs=(tokens, tokens, tokens, tokens, P()),
        out_specs=(tokens, tokens, tokens, tokens),
        check_vma=False,
    )
```

```python
import math

import jax
import jax.numpy as jnp
from jax import lax
from jax.experimental import pallas as pl
from jax.experimental.pallas import tpu as pltpu
from jax.sharding import Mesh
from jax.sharding import PartitionSpec as P

AXES = ("x", "y", "l", "h", "k", "c")
SIZES = (4, 8, 2, 2, 2, 2)
RING = ("l", "h", "k")
COLUMNS = ("x", "y")

HD = 128
KVH = 8
GROUP = 8
TOK = 32
COL = 512
REACH = 2
KEYS = (REACH + 1) * COL
PIECE = TOK * GROUP
TILE = 128
PAIR = 2
ROWS = PAIR * PIECE
BLOCKS = KVH // PAIR
PLACES = [
    sum((p >> ("k", "h", "l").index(axis) & 1) << (2 - n) for n, axis in enumerate(RING)) for p in range(KVH)
]
WIN = 9
NEAR = WIN - BLOCKS
SCALE = HD**-0.5
SCALE2 = SCALE * math.log2(math.e)
NEG = -1e30

F32 = jnp.float32
BF16 = jnp.bfloat16
VMEM = pl.BlockSpec(memory_space=pltpu.VMEM)
SMEM = pl.BlockSpec(memory_space=pltpu.SMEM)
HBM = pl.BlockSpec(memory_space=pl.ANY)
NT = (((1,), (1,)), ((), ()))
NN = (((1,), (0,)), ((), ()))


def dot(a, b, dims):
    return lax.dot_general(a, b, dims, preferred_element_type=F32)


def call(kernel, outs, ins, scratch, name, flops=0, nbytes=1 << 20, first=VMEM):
    return pl.pallas_call(
        kernel,
        out_shape=outs,
        in_specs=ins,
        out_specs=[first] + [VMEM] * (len(outs) - 1),
        scratch_shapes=scratch,
        compiler_params=pltpu.CompilerParams(vmem_limit_bytes=48 << 20),
        cost_estimate=pl.CostEstimate(flops=flops, bytes_accessed=nbytes, transcendentals=0),
        name=name,
    )


def shape(*dims, dtype=BF16):
    return jax.ShapeDtypeStruct(dims, dtype)


def put_heads(x_ref, out_ref, at):
    for pair in range(KVH // 2):
        both = x_ref[:, pair * 2 * GROUP : (pair + 1) * 2 * GROUP, :].astype(F32)
        for part in range(2):
            half = both[:, part * GROUP : (part + 1) * GROUP, :]
            out_ref[2 * pair + part, at : at + PIECE, :] = half.reshape(PIECE, HD).astype(BF16)


def take_heads(x_ref, at, out_ref):
    for pair in range(KVH // 2):
        halves = [
            x_ref[2 * pair + part, at : at + PIECE, :].astype(F32).reshape(TOK, GROUP, HD)
            for part in range(2)
        ]
        both = jnp.concatenate(halves, axis=1).astype(BF16)
        out_ref[:, pair * 2 * GROUP : (pair + 1) * 2 * GROUP, :] = both


def pack_qg(q_ref, g_ref, out_ref):
    put_heads(q_ref, out_ref, 0)
    put_heads(g_ref, out_ref, PIECE)


def unpack_od(x_ref, out_ref, dq_ref):
    take_heads(x_ref, 0, out_ref)
    take_heads(x_ref, PIECE, dq_ref)


def unpack_kv(x_ref, k_ref, v_ref, wide):
    for at, ref in ((0, k_ref), (TOK, v_ref)):
        for j in range(KVH):
            wide[pl.ds(j, TOK, stride=KVH), :] = x_ref[j, at : at + TOK, :].astype(F32)
        ref[...] = wide[...].reshape(TOK, KVH, HD).astype(BF16)


def attend(where_ref, qg_ref, start_ref, own_ref, other_ref, old_ref, other_old_ref,
           od_ref, mine_ref, theirs_ref,
           keys, values, keys_t, values_t, scores, probs, dscores, dk, dv, od, sems):
    core = where_ref[0]
    for column in range(REACH + 1):
        for piece in range(KVH):
            base = (REACH - column) * COL + piece * 2 * TOK
            for ref, old, which in ((own_ref, old_ref, core), (other_ref, other_old_ref, 1 - core)):
                at = pl.ds(pl.multiple_of(base + which * TOK, TOK), TOK)
                got = ref[PLACES[piece]] if column == 0 else old[column - 1, PLACES[piece]]
                keys[at, :] = got[0:TOK]
                values[at, :] = got[TOK : 2 * TOK]
    for t in range(KEYS // TILE):
        at = slice(t * TILE, (t + 1) * TILE)
        keys_t[:, at] = jnp.transpose(keys[at, :])
        values_t[:, at] = jnp.transpose(values[at, :])
    dk[...] = jnp.zeros(dk.shape, F32)
    dv[...] = jnp.zeros(dv.shape, F32)
    index = lax.broadcasted_iota(jnp.int32, (TILE, ROWS), 0)
    row = lax.broadcasted_iota(jnp.int32, (1, ROWS), 1)
    inside = (row // PIECE) * (2 * TOK) + core * TOK + (row % PIECE) // GROUP

    tiles = [slice(t * TILE, (t + 1) * TILE) for t in range(WIN)]

    class Block:
        def __init__(self, at, count, sent):
            self.sent = sent
            self.slot = at % 2
            self.count = count
            self.base = (at + WIN - count) * TILE
            self.window = slice(self.base, self.base + count * TILE)
            self.held = slice(0, count * TILE)
            self.pieces = PLACES[at * PAIR : (at + 1) * PAIR]
            self.q = jnp.concatenate([qg_ref[p, 0:PIECE, :] for p in self.pieces], axis=0)
            self.g = jnp.concatenate([qg_ref[p, PIECE : 2 * PIECE, :] for p in self.pieces], axis=0)
            self.g_t = jnp.transpose(self.g.astype(F32))
            self.start = start_ref[at] - self.base
            self.top = jnp.full((8, ROWS), NEG, F32)
            self.sums = jnp.zeros((8, ROWS), F32)

        def keys_of(self, t):
            return slice(self.base + t * TILE, self.base + (t + 1) * TILE)

        def put(self, at, result):
            rows = jnp.transpose(result).astype(BF16)
            for n, p in enumerate(self.pieces):
                piece = (p, pl.ds(at, PIECE))
                od[piece] = rows[n * PIECE : (n + 1) * PIECE]
                copy = pltpu.make_async_copy(od.at[piece], od_ref.at[piece], sems.at[len(self.sent)])
                copy.start()
                self.sent.append(copy)

        def score(self, t):
            s = dot(keys[self.keys_of(t), :], self.q, NT)
            seen = index >= self.start - t * TILE
            if t == self.count - 1:
                seen = seen & (index <= inside)
            s = jnp.where(seen, s, NEG)
            scores[tiles[t], :] = s
            self.top = jnp.maximum(self.top, jnp.max(s.reshape(TILE // 8, 8, ROWS), axis=0))

        def find_top(self):
            self.row_top = jnp.max(self.top, axis=0, keepdims=True) * SCALE2

        def weigh(self, t):
            p = jnp.exp2(scores[tiles[t], :] * SCALE2 - self.row_top)
            self.sums = self.sums + jnp.sum(p.reshape(TILE // 8, 8, ROWS), axis=0)
            probs[self.slot, tiles[t], :] = p.astype(BF16)

        def output(self):
            self.inv = 1.0 / jnp.sum(self.sums, axis=0, keepdims=True)
            out = dot(values_t[:, self.window], probs[self.slot, self.held], NN) * self.inv
            self.drift = jnp.sum(out * self.g_t, axis=0, keepdims=True)
            self.put(0, out)
            self.g_scaled = jnp.transpose((self.g_t * self.inv).astype(BF16))

        def dscore(self, t):
            dp = dot(values[self.keys_of(t), :], self.g, NT)
            ds = ((dp - self.drift) * self.inv).astype(BF16)
            dscores[self.slot, tiles[t], :] = ds * probs[self.slot, tiles[t], :]

        def dvalue(self):
            dv[self.window, :] += dot(probs[self.slot, self.held], self.g_scaled, NN)

        def dkey(self):
            dk[self.window, :] += dot(dscores[self.slot, self.held], self.q, NN)

        def dquery(self):
            self.put(PIECE, dot(keys_t[:, self.window], dscores[self.slot, self.held], NN) * SCALE)

    def pipeline(counts):
        last = None
        sent = []
        for at in range(BLOCKS + 1):
            block = Block(at, counts[at], sent) if at < BLOCKS else None
            for t in range(WIN):
                if block and t < block.count:
                    block.score(t)
                if last and t < last.count:
                    last.dscore(t)
            if block:
                block.find_top()
            if last:
                last.dvalue()
            for t in range(WIN):
                if block and t < block.count:
                    block.weigh(t)
            if last:
                last.dkey()
                last.dquery()
            if block:
                block.output()
            last = block
        for copy in sent:
            copy.wait()

    @pl.when(where_ref[1] != 0)
    def far():
        pipeline([WIN] * (BLOCKS - 1) + [BLOCKS])

    @pl.when(where_ref[1] == 0)
    def near():
        pipeline([NEAR + 1 + at for at in range(BLOCKS)])

    for column in range(REACH + 1):
        for piece in range(KVH):
            base = (REACH - column) * COL + piece * 2 * TOK
            for ref, which in ((mine_ref, core), (theirs_ref, 1 - core)):
                at = pl.ds(pl.multiple_of(base + which * TOK, TOK), TOK)
                ref[column, PLACES[piece], 0:TOK] = (dk[at, :] * SCALE).astype(ref.dtype)
                ref[column, PLACES[piece], TOK : 2 * TOK] = dv[at, :].astype(ref.dtype)


def old_terms(mine_ref, got_ref, one_ref, two_ref):
    one_ref[...] = (mine_ref[1] + got_ref[1].astype(F32)).astype(BF16)
    two_ref[...] = (mine_ref[2] + got_ref[2].astype(F32)).astype(BF16)


def add_terms(mine_ref, got_ref, one_ref, two_ref, out_ref):
    out_ref[...] = (
        mine_ref[0] + got_ref[0].astype(F32) + one_ref[...].astype(F32) + two_ref[...].astype(F32)
    ).astype(BF16)


def exchange(x):
    return lax.all_to_all(x, RING, split_axis=0, concat_axis=0, tiled=True)


def shifted(x, by):
    count = SIZES[0] * SIZES[1]
    return lax.ppermute(x, COLUMNS, [(i, (i + by) % count) for i in range(count)])


def swapped(x):
    return lax.ppermute(x, "c", [(0, 1), (1, 0)])


def starts(doc_lengths, column, core):
    ends = jnp.cumsum(doc_lengths)
    row = jnp.arange(ROWS, dtype=jnp.int32)
    piece = jnp.arange(BLOCKS, dtype=jnp.int32)[:, None] * PAIR + (row // PIECE)[None, :]
    place = column * COL + piece * (2 * TOK) + core * TOK + ((row % PIECE) // GROUP)[None, :]
    start = jnp.max(jnp.where(ends[:, None, None] <= place[None], ends[:, None, None], 0), axis=0)
    return jnp.maximum(start - (column - REACH) * COL, 0).astype(jnp.int32)[:, None, :]


def shards(query_in, key_in, value_in, grad_out, doc_lengths):
    both_kv = shape(KVH, 2 * TOK, HD)
    both_wide = shape(KVH, 2 * PIECE, HD)
    heads_kv = shape(TOK, KVH, HD)
    heads_wide = shape(TOK, KVH * GROUP, HD)
    wide = [pltpu.VMEM((TOK * KVH, HD), F32)]

    packed = jnp.transpose(jnp.concatenate([key_in, value_in], axis=0), (1, 0, 2))
    kv = exchange(packed)
    qg = exchange(call(pack_qg, [both_wide], [VMEM] * 2, [], "pack_qg")(query_in, grad_out)[0])
    other = swapped(kv)
    old = jnp.stack([shifted(kv, 1), shifted(kv, 2)])
    old, other = lax.optimization_barrier((old, other))
    other_old = swapped(old)

    core = lax.axis_index("c").astype(jnp.int32)
    start = starts(doc_lengths, lax.axis_index(COLUMNS), core)
    where = jnp.stack([core, (start[0, 0, 0] < REACH * COL - NEAR * TILE).astype(jnp.int32)])
    od, mine, theirs = call(
        attend,
        [both_wide, shape(REACH + 1, KVH, 2 * TOK, HD, dtype=F32), shape(REACH + 1, KVH, 2 * TOK, HD)],
        [SMEM] + [VMEM] * 6,
        [pltpu.VMEM((KEYS, HD), BF16)] * 2
        + [pltpu.VMEM((HD, KEYS), BF16)] * 2
        + [pltpu.VMEM((WIN * TILE, ROWS), F32)]
        + [pltpu.VMEM((2, WIN * TILE, ROWS), BF16)] * 2
        + [pltpu.VMEM((KEYS, HD), F32)] * 2
        + [pltpu.VMEM((KVH, 2 * PIECE, HD), BF16), pltpu.SemaphoreType.DMA((4 * BLOCKS,))],
        "attend",
        12 * BLOCKS * ROWS * WIN * TILE * HD,
        first=HBM,
    )(where, qg, start, kv, other, old, other_old)

    od_back = exchange(od)
    got = swapped(theirs)
    one, two = call(old_terms, [both_kv] * 2, [VMEM] * 2, [], "old_terms")(mine, got)
    one, two = shifted(one, -1), shifted(two, -2)
    total = call(add_terms, [both_kv], [VMEM] * 4, [], "add_terms")(mine, got, one, two)[0]
    od_back, total = lax.optimization_barrier((od_back, total))
    grads_kv = exchange(total)
    attn_out, grad_query = call(unpack_od, [heads_wide] * 2, [VMEM], [], "unpack_od")(od_back)
    grad_key, grad_value = call(unpack_kv, [heads_kv] * 2, [VMEM], wide, "unpack_kv")(grads_kv)
    return (attn_out, grad_query, grad_key, grad_value)


def solution(mesh):
    fine = Mesh(mesh.devices.reshape(SIZES), AXES)
    tokens = P(AXES, None, None)
    return jax.shard_map(
        shards,
        mesh=fine,
        in_specs=(tokens, tokens, tokens, tokens, P()),
        out_specs=(tokens, tokens, tokens, tokens),
        check_vma=False,
    )
```
